1024 devices in a mesh: row: 32 (over z, y_hi), col: 32 (over y_lo, x, core).
Axes of the slice: x: 4, y: 8 (y_hi: 2, y_lo: 4; y = y_hi * 4 + y_lo), z: 16, core: 2. Of those that a mesh axis runs over, the one named last changes fastest.
Arguments:
- pmi: bfloat16 [32768, 32768], P('col', 'row'), may hold values from -0.03125 to 0.03125
- tile_mask: int32 [256, 256], P('col', 'row'), may hold values 0 or 1
- probe: bfloat16 [32768, 256], P('row', 'col'), may hold values from -6 to 6
Outputs:
- basis: float32 [32768, 256], P(('row', 'col'))
- factor: float32 [256, 256], replicated
The draws below stay inside these ranges and needn't reach their ends.
All inputs are finite; a program needn't handle non-finite values. No bound on the sum of `tile_mask` on one device may be relied on, other than what follows from the above.
Results may differ from the reference program's by a relative error of at most 0.0021.
Values may be sent and summed in bfloat16 or wider, within the bound.
No kernel may reach another device: no remote copies, remote signals or barrier semaphores. Data moves between devices by JAX's collectives and lax.ppermute only.
A program may use at most 32 MiB of HBM per device.

```python
import math
import jax
import jax.numpy as jnp
from jax import lax

TILE = 128
K = 256
M = 32768
NC = 32768


def place_ends(result, rng, smallest, largest):
    dims = result.shape
    index_at = [jax.random.randint(jax.random.fold_in(rng, axis), (), 0, dims[axis]) for axis in range(len(dims))]
    result = result.at[tuple(index_at)].set(smallest)
    longest = dims.index(max(dims))
    index_at[longest] = (index_at[longest] + 1) % dims[longest]
    return result.at[tuple(index_at)].set(largest)


def shard_levels(rng, shape, split, least, high):
    def one(axis_at, blocks):
        steps = jax.random.uniform(jax.random.fold_in(jax.random.fold_in(rng, 6), axis_at), (blocks,), jnp.float32, least / len(split), high / len(split))
        return jnp.repeat(jnp.exp(steps), shape[axis_at] // blocks).reshape((-1,) + (1,) * (len(shape) - axis_at - 1))

    level = one(*split[0])
    for cut in split[1:]:
        level = level * one(*cut)
    return level


def scatter_about(stream_key, extent, spread, bound, cuts=(), dtype=jnp.bfloat16):
    result = jax.random.normal(stream_key, extent, jnp.float32) * spread
    if len(cuts) > 0:
        result = shard_levels(stream_key, extent, cuts, -0.22, 0.18) * result
    return jnp.clip(result, min=-bound, max=bound).astype(dtype)


def setup_inputs(seed: int = 0) -> dict:
    splits = jax.random.split(jax.random.key(seed), 4)
    return {
        "pmi": scatter_about(splits[0], (M, NC), NC ** -0.5, 0.03125, ((0, 32), (1, 32))),
        "tile_mask": place_ends((jax.random.randint(splits[1], (M // TILE, NC // TILE), 0, 2) < 1).astype(jnp.int32), jax.random.fold_in(splits[1], 1), 0, 1),
        "probe": scatter_about(splits[2], (NC, K), 1.0, 6.0, ((0, 32), (1, 32))),
    }


def reference(pmi, tile_mask, probe):
    scaled = tile_mask.astype(jnp.bfloat16)[:, None, :, None]
    masked = (pmi.reshape(M // TILE, TILE, NC // TILE, TILE) * scaled).reshape(M, NC)
    sketch = jnp.dot(masked.astype(jnp.float32), probe.astype(jnp.float32), preferred_element_type=jnp.float32).astype(jnp.bfloat16)
    image = jnp.dot(sketch.T.astype(jnp.float32), masked.astype(jnp.float32), preferred_element_type=jnp.float32).T
    gram = jnp.dot(image.T.astype(jnp.float32), image.astype(jnp.float32), precision=lax.Precision.HIGHEST, preferred_element_type=jnp.float32)
    lower = jnp.linalg.cholesky(gram)
    solved = lax.linalg.triangular_solve(lower, image, left_side=False, lower=True, transpose_a=True)
    basis = solved * jnp.float32(math.sqrt(NC))
    return (basis, lower.T)
```

```python
import functools
import math

import jax
import jax.numpy as jnp
from jax import lax
from jax.experimental import pallas as pl
from jax.experimental.pallas import tpu as pltpu
from jax.sharding import PartitionSpec as P

TILE = 128


def exchange(blocks, axis):
    return lax.all_to_all(blocks, axis, split_axis=0, concat_axis=0, tiled=True)


def spread(block, axis):
    n = lax.axis_size(axis)
    return exchange(jnp.broadcast_to(block[None], (n,) + block.shape), axis)


def scatter_sum(whole, axis):
    n = lax.axis_size(axis)
    rows, columns = whole.shape
    return jnp.sum(exchange(whole.reshape(n, rows // n, columns), axis), axis=0)

SUB = 8
LANES = 128
PANEL = 64


def eliminate(panel, first):
    height, width = panel.shape
    tiles = height // SUB
    rows = [panel[SUB * v : SUB * (v + 1)] for v in range(tiles)]
    sub = lax.broadcasted_iota(jnp.int32, (SUB, LANES), 0)

    def wide(a):
        return jnp.concatenate([a] * (width // LANES), axis=1)

    done = []
    for t in range(tiles):
        at = first + t * SUB
        pivots = jnp.zeros((SUB, LANES), jnp.float32)
        columns = {
            v: [jnp.broadcast_to(rows[v][:, at + k : at + k + 1], (SUB, LANES)) for k in range(SUB)]
            for v in range(t, tiles)
        }
        for k in range(SUB):
            pivot = jnp.broadcast_to(columns[t][k][k : k + 1], (SUB, LANES))
            inverse = 1.0 / pivot
            pivots = jnp.where(sub == k, pivot, pivots)
            row = jnp.broadcast_to(rows[t][k : k + 1], (SUB, width))
            heads = [jnp.broadcast_to(columns[t][l][k : k + 1], (SUB, LANES)) for l in range(k + 1, SUB)]
            for v in range(t, tiles):
                times = columns[v][k] * inverse
                if v == t:
                    times = jnp.where(sub > k, times, 0.0)
                rows[v] = rows[v] - wide(times) * row
                for l in range(k + 1, SUB):
                    columns[v][l] = columns[v][l] - times * heads[l - k - 1]
        done.append(rows[t] * wide(lax.rsqrt(pivots)))
    return jnp.concatenate(done, axis=0)


def cholesky_qr_kernel(scale, gram_ref, right_ref, factor_ref, basis_ref, work):
    n, size = right_ref.shape
    padding = jnp.zeros((LANES - n, size), jnp.float32)
    work[:, :size] = gram_ref[...]
    work[:, size:] = jnp.concatenate([right_ref[...], padding], axis=0).T
    for low in range(0, size, PANEL):
        high = low + PANEL
        panel = eliminate(work[low:high, :], low)
        work[low:high, :] = panel
        if high < size:
            base = high // LANES * LANES
            change = lax.dot_general(
                panel[:, base:size],
                panel,
                (((0,), (0,)), ((), ())),
                precision=lax.Precision.HIGHEST,
                preferred_element_type=jnp.float32,
            )
            work[high:, :] = work[high:, :] - change[high - base :]
    at_row = lax.broadcasted_iota(jnp.int32, (size, size), 0)
    at_column = lax.broadcasted_iota(jnp.int32, (size, size), 1)
    factor_ref[...] = jnp.where(at_row <= at_column, work[:, :size], 0.0)
    basis_ref[...] = work[:, size:].T[:n] * scale


def cholesky_qr(gram, right, scale):
    vmem = pl.BlockSpec(memory_space=pltpu.VMEM)
    size = gram.shape[0]
    return pl.pallas_call(
        functools.partial(cholesky_qr_kernel, scale),
        out_shape=(
            jax.ShapeDtypeStruct((size, size), jnp.float32),
            jax.ShapeDtypeStruct(right.shape, jnp.float32),
        ),
        in_specs=[vmem, vmem],
        out_specs=(vmem, vmem),
        scratch_shapes=[pltpu.VMEM((size, size + LANES), jnp.float32)],
        name="cholesky_qr",
    )(gram, right)


def local(pmi, tile_mask, probe):
    rows, cols = pmi.shape
    scaled = tile_mask.astype(jnp.bfloat16)[:, None, :, None]
    masked = (pmi.reshape(rows // TILE, TILE, cols // TILE, TILE) * scaled).reshape(rows, cols)
    probe_full = spread(probe.T, "col").reshape(-1, cols)
    k = probe_full.shape[0]
    partial_value = lax.dot_general(
        masked, probe_full, (((1,), (1,)), ((), ())), preferred_element_type=jnp.float32
    )
    sketch_rows = scatter_sum(partial_value, "row").astype(jnp.bfloat16)
    sketch = spread(sketch_rows, "row").reshape(rows, k)
    image = lax.dot_general(
        masked, sketch, (((0,), (0,)), ((), ())), preferred_element_type=jnp.float32
    )
    mine = scatter_sum(image, "col")
    gram_part = jnp.dot(
        mine.T, mine, precision=lax.Precision.HIGHEST, preferred_element_type=jnp.float32
    )
    gram_rows = jnp.sum(spread(scatter_sum(gram_part, "col"), "row"), axis=0)
    gram = spread(gram_rows, "col").reshape(k, k)
    scale = math.sqrt(cols * lax.axis_size("row"))
    factor, basis = cholesky_qr(gram, mine, scale)
    return (basis, factor)


def solution(mesh):
    in_specs = (P("col", "row"), P("col", "row"), P("row", "col"))
    out_specs = (P(("row", "col"), None), P())
    return jax.shard_map(local, mesh=mesh, in_specs=in_specs, out_specs=out_specs, check_vma=False)
```

```python
import functools
import math

import jax
import jax.numpy as jnp
from jax import lax
from jax.experimental import pallas as pl
from jax.experimental.pallas import tpu as pltpu
from jax.sharding import Mesh
from jax.sharding import PartitionSpec as P

TILE = 128


Z, Y, CHIP, CORE = "z", "y_hi", ("y_lo", "x"), "core"
ROW, COL = (Z, Y), CHIP + (CORE,)
LIMIT = 32767.0


def exchange(blocks, axis):
    return lax.all_to_all(blocks, axis, split_axis=0, concat_axis=0, tiled=True)


def spread(block, axis):
    n = lax.axis_size(axis)
    return exchange(jnp.broadcast_to(block[None], (n,) + block.shape), axis)


def swap(block, axis):
    return lax.ppermute(block, axis, [(0, 1), (1, 0)])


def scatter_sum(whole, axis):
    n = lax.axis_size(axis)
    rows, columns = whole.shape
    return jnp.sum(exchange(whole.reshape(n, rows // n, columns), axis), axis=0)


def scatter_sum_16(whole, axis):
    n = lax.axis_size(axis)
    rows, columns = whole.shape
    pieces = whole.reshape(n, rows // n, columns)
    top = jnp.max(jnp.abs(pieces), axis=1, keepdims=True)
    power = jnp.ceil(jnp.log2(jnp.maximum(top, 1e-30)) + 0.001)
    coded = jnp.round(pieces * (jnp.exp2(-power) * LIMIT)).astype(jnp.int16)
    powers = jnp.broadcast_to(power.astype(jnp.int16), (n, 8, columns))
    came = exchange(jnp.concatenate([coded, powers], axis=1), axis)
    unit = jnp.exp2(came[:, -1:].astype(jnp.float32)) * (1 / LIMIT)
    return jnp.sum(came[:, :-8].astype(jnp.float32) * unit, axis=0)


def chip_scatter_sum(whole):
    n = lax.axis_size(CHIP)
    rows, columns = whole.shape
    halves = whole.reshape(n, 2, rows // (2 * n), columns)
    core = lax.axis_index(CORE)
    mine = lax.dynamic_index_in_dim(halves, core, axis=1, keepdims=False)
    other = lax.dynamic_index_in_dim(halves, 1 - core, axis=1, keepdims=False)
    return jnp.sum(exchange(mine + swap(other, CORE), CHIP), axis=0)


def chip_spread(block):
    mine = spread(block, CHIP)
    other = swap(mine, CORE)
    first = lax.axis_index(CORE) == 0
    both = jnp.stack([jnp.where(first, mine, other), jnp.where(first, other, mine)], axis=1)
    return both.reshape((-1,) + block.shape)


SUB = 8
LANES = 128
PANEL = 64


def eliminate(panel, first):
    height, width = panel.shape
    tiles = height // SUB
    rows = [panel[SUB * v : SUB * (v + 1)] for v in range(tiles)]
    sub = lax.broadcasted_iota(jnp.int32, (SUB, LANES), 0)

    def wide(a):
        return jnp.concatenate([a] * (width // LANES), axis=1)

    done = []
    for t in range(tiles):
        at = first + t * SUB
        pivots = jnp.zeros((SUB, LANES), jnp.float32)
        columns = {
            v: [jnp.broadcast_to(rows[v][:, at + k : at + k + 1], (SUB, LANES)) for k in range(SUB)]
            for v in range(t, tiles)
        }
        for k in range(SUB):
            pivot = jnp.broadcast_to(columns[t][k][k : k + 1], (SUB, LANES))
            inverse = 1.0 / pivot
            pivots = jnp.where(sub == k, pivot, pivots)
            row = jnp.broadcast_to(rows[t][k : k + 1], (SUB, width))
            heads = [jnp.broadcast_to(columns[t][l][k : k + 1], (SUB, LANES)) for l in range(k + 1, SUB)]
            for v in range(t, tiles):
                times = columns[v][k] * inverse
                if v == t:
                    times = jnp.where(sub > k, times, 0.0)
                rows[v] = rows[v] - wide(times) * row
                for l in range(k + 1, SUB):
                    columns[v][l] = columns[v][l] - times * heads[l - k - 1]
        done.append(rows[t] * wide(lax.rsqrt(pivots)))
    return jnp.concatenate(done, axis=0)


def cholesky_qr_kernel(scale, gram_ref, right_ref, factor_ref, basis_ref, work):
    n, size = right_ref.shape
    padding = jnp.zeros((LANES - n, size), jnp.float32)
    work[:, :size] = gram_ref[...]
    work[:, size:] = jnp.concatenate([right_ref[...], padding], axis=0).T
    for low in range(0, size, PANEL):
        high = low + PANEL
        panel = eliminate(work[low:high, :], low)
        work[low:high, :] = panel
        if high < size:
            base = high // LANES * LANES
            change = lax.dot_general(
                panel[:, base:size],
                panel,
                (((0,), (0,)), ((), ())),
                precision=lax.Precision.HIGHEST,
                preferred_element_type=jnp.float32,
            )
            work[high:, :] = work[high:, :] - change[high - base :]
    at_row = lax.broadcasted_iota(jnp.int32, (size, size), 0)
    at_column = lax.broadcasted_iota(jnp.int32, (size, size), 1)
    factor_ref[...] = jnp.where(at_row <= at_column, work[:, :size], 0.0)
    basis_ref[...] = work[:, size:].T[:n] * scale


def cholesky_qr(gram, right, scale):
    vmem = pl.BlockSpec(memory_space=pltpu.VMEM)
    size = gram.shape[0]
    return pl.pallas_call(
        functools.partial(cholesky_qr_kernel, scale),
        out_shape=(
            jax.ShapeDtypeStruct((size, size), jnp.float32),
            jax.ShapeDtypeStruct(right.shape, jnp.float32),
        ),
        in_specs=[vmem, vmem],
        out_specs=(vmem, vmem),
        scratch_shapes=[pltpu.VMEM((size, size + LANES), jnp.float32)],
        name="cholesky_qr",
    )(gram, right)


def local(pmi, tile_mask, probe):
    rows, cols = pmi.shape
    scaled = tile_mask.astype(jnp.bfloat16)[:, None, :, None]
    masked = (pmi.reshape(rows // TILE, TILE, cols // TILE, TILE) * scaled).reshape(rows, cols)
    probe_full = chip_spread(probe.T).reshape(-1, cols)
    k = probe_full.shape[0]
    partial_value = lax.dot_general(
        masked, probe_full, (((1,), (1,)), ((), ())), preferred_element_type=jnp.float32
    )
    sketch_rows = scatter_sum_16(partial_value, Z)
    sketch_rows = (sketch_rows + swap(sketch_rows, Y)).astype(jnp.bfloat16)
    sketch = spread(sketch_rows, Z).reshape(rows, k)
    image = lax.dot_general(
        masked, sketch, (((0,), (0,)), ((), ())), preferred_element_type=jnp.float32
    )
    mine = chip_scatter_sum(image)
    gram_part = jnp.dot(
        mine.T, mine, precision=lax.Precision.HIGHEST, preferred_element_type=jnp.float32
    )
    gram_rows = jnp.sum(spread(scatter_sum(gram_part, COL), ROW), axis=0)
    gram = spread(gram_rows, COL).reshape(k, k)
    scale = math.sqrt(cols * lax.axis_size(ROW))
    factor, basis = cholesky_qr(gram, mine, scale)
    return (basis, factor)


def solution(mesh):
    sizes = (mesh.shape["row"] // 2, 2, 4, mesh.shape["col"] // 8, 2)
    parts = Mesh(mesh.devices.reshape(sizes), ROW + COL)
    in_specs = (P(COL, ROW), P(COL, ROW), P(ROW, COL))
    out_specs = (P(ROW + COL, None), P())
    return jax.shard_map(local, mesh=parts, in_specs=in_specs, out_specs=out_specs, check_vma=False)
```

```python
import functools
import math

import jax
import jax.numpy as jnp
from jax import lax
from jax.experimental import pallas as pl
from jax.experimental.pallas import tpu as pltpu
from jax.sharding import Mesh
from jax.sharding import PartitionSpec as P

TILE = 128


Z, Y, CHIP, CORE = "z", "y_hi", ("y_lo", "x"), "core"
ROW, COL, PLANE = (Z, Y), CHIP + (CORE,), (Y,) + CHIP
LIMIT = 32767.0


def exchange(blocks, axis):
    return lax.all_to_all(blocks, axis, split_axis=0, concat_axis=0, tiled=True)


def spread(block, axis):
    n = lax.axis_size(axis)
    return exchange(jnp.broadcast_to(block[None], (n,) + block.shape), axis)


def swap(block, axis):
    return lax.ppermute(block, axis, [(0, 1), (1, 0)])


def scatter_sum(whole, axis):
    n = lax.axis_size(axis)
    rows, columns = whole.shape
    return jnp.sum(exchange(whole.reshape(n, rows // n, columns), axis), axis=0)


def scatter_sum_16(pieces, axis):
    n, _, columns = pieces.shape
    top = jnp.max(jnp.abs(pieces), axis=1, keepdims=True)
    power = jnp.ceil(jnp.log2(jnp.maximum(top, 1e-30)) + 0.001)
    coded = jnp.round(pieces * (jnp.exp2(-power) * LIMIT)).astype(jnp.int16)
    powers = jnp.broadcast_to(power.astype(jnp.int16), (n, 8, columns))
    came = exchange(jnp.concatenate([coded, powers], axis=1), axis)
    unit = jnp.exp2(came[:, -1:].astype(jnp.float32)) * (1 / LIMIT)
    return jnp.sum(came[:, :-8].astype(jnp.float32) * unit, axis=0)


def chip_scatter_sum(whole):
    n = lax.axis_size(CHIP)
    rows, columns = whole.shape
    halves = whole.reshape(n, 2, rows // (2 * n), columns)
    core = lax.axis_index(CORE)
    mine = lax.dynamic_index_in_dim(halves, core, axis=1, keepdims=False)
    other = lax.dynamic_index_in_dim(halves, 1 - core, axis=1, keepdims=False)
    return scatter_sum_16(mine + swap(other, CORE), CHIP)


def chip_spread(block):
    mine = spread(block, CHIP)
    other = swap(mine, CORE)
    first = lax.axis_index(CORE) == 0
    both = jnp.stack([jnp.where(first, mine, other), jnp.where(first, other, mine)], axis=1)
    return both.reshape((-1,) + block.shape)


SUB = 8
LANES = 128
PANEL = 64


def eliminate(panel, first):
    height, width = panel.shape
    tiles = height // SUB
    rows = [panel[SUB * v : SUB * (v + 1)] for v in range(tiles)]
    sub = lax.broadcasted_iota(jnp.int32, (SUB, LANES), 0)

    def wide(a):
        return jnp.concatenate([a] * (width // LANES), axis=1)

    done = []
    for t in range(tiles):
        at = first + t * SUB
        pivots = jnp.zeros((SUB, LANES), jnp.float32)
        columns = {
            v: [jnp.broadcast_to(rows[v][:, at + k : at + k + 1], (SUB, LANES)) for k in range(SUB)]
            for v in range(t, tiles)
        }
        for k in range(SUB):
            pivot = jnp.broadcast_to(columns[t][k][k : k + 1], (SUB, LANES))
            inverse = 1.0 / pivot
            pivots = jnp.where(sub == k, pivot, pivots)
            row = jnp.broadcast_to(rows[t][k : k + 1], (SUB, width))
            heads = [jnp.broadcast_to(columns[t][l][k : k + 1], (SUB, LANES)) for l in range(k + 1, SUB)]
            for v in range(t, tiles):
                times = columns[v][k] * inverse
                if v == t:
                    times = jnp.where(sub > k, times, 0.0)
                rows[v] = rows[v] - wide(times) * row
                for l in range(k + 1, SUB):
                    columns[v][l] = columns[v][l] - times * heads[l - k - 1]
        done.append(rows[t] * wide(lax.rsqrt(pivots)))
    return jnp.concatenate(done, axis=0)


def cholesky_qr_kernel(scale, gram_ref, right_ref, factor_ref, basis_ref, work):
    n, size = right_ref.shape
    work[:, :size] = gram_ref[...]
    right = right_ref[...]
    if n < LANES:
        right = jnp.concatenate([right, jnp.zeros((LANES - n, size), jnp.float32)], axis=0)
    work[:, size:] = right.T
    for low in range(0, size, PANEL):
        high = low + PANEL
        panel = eliminate(work[low:high, :], low)
        work[low:high, :] = panel
        if high < size:
            base = high // LANES * LANES
            change = lax.dot_general(
                panel[:, base:size],
                panel,
                (((0,), (0,)), ((), ())),
                precision=lax.Precision.HIGHEST,
                preferred_element_type=jnp.float32,
            )
            work[high:, :] = work[high:, :] - change[high - base :]
    at_row = lax.broadcasted_iota(jnp.int32, (size, size), 0)
    at_column = lax.broadcasted_iota(jnp.int32, (size, size), 1)
    factor_ref[...] = jnp.where(at_row <= at_column, work[:, :size], 0.0)
    basis_ref[...] = work[:, size:].T[:n] * scale


def cholesky_qr(gram, right, scale):
    vmem = pl.BlockSpec(memory_space=pltpu.VMEM)
    size = gram.shape[0]
    return pl.pallas_call(
        functools.partial(cholesky_qr_kernel, scale),
        out_shape=(
            jax.ShapeDtypeStruct((size, size), jnp.float32),
            jax.ShapeDtypeStruct(right.shape, jnp.float32),
        ),
        in_specs=[vmem, vmem],
        out_specs=(vmem, vmem),
        scratch_shapes=[pltpu.VMEM((size, size + LANES), jnp.float32)],
        name="cholesky_qr",
    )(gram, right)


def masked(pmi, tile_mask):
    rows, cols = pmi.shape
    scaled = tile_mask.astype(jnp.bfloat16)[:, None, :, None]
    return (pmi.reshape(rows // TILE, TILE, cols // TILE, TILE) * scaled).reshape(rows, cols)


def local(pmi, tile_mask, probe):
    rows, cols = pmi.shape
    again, mask_again = lax.optimization_barrier((pmi, tile_mask))
    probe_full = chip_spread(probe.T).reshape(-1, cols)
    k = probe_full.shape[0]
    partial_value = lax.dot_general(
        masked(pmi, tile_mask), probe_full, (((1,), (1,)), ((), ())), preferred_element_type=jnp.float32
    )
    sketch_rows = scatter_sum_16(partial_value.reshape(lax.axis_size(Z), -1, k), Z)
    sketch_rows = (sketch_rows + swap(sketch_rows, Y)).astype(jnp.bfloat16)
    sketch = spread(sketch_rows, Z).reshape(rows, k)
    image = lax.dot_general(
        masked(again, mask_again), sketch, (((0,), (0,)), ((), ())), preferred_element_type=jnp.float32
    )
    mine = chip_scatter_sum(image)
    gram_part = jnp.dot(
        mine.T, mine, precision=lax.Precision.HIGHEST, preferred_element_type=jnp.float32
    )
    gram_rows = jnp.sum(spread(scatter_sum(gram_part, PLANE), (Z, CORE)), axis=0)
    gram = spread(gram_rows, PLANE).reshape(k, k)
    scale = math.sqrt(cols * lax.axis_size(ROW))
    factor, basis = cholesky_qr(gram, mine, scale)
    return (basis, factor)


def solution(mesh):
    sizes = (mesh.shape["row"] // 2, 2, 4, mesh.shape["col"] // 8, 2)
    parts = Mesh(mesh.devices.reshape(sizes), ROW + COL)
    in_specs = (P(COL, ROW), P(COL, ROW), P(ROW, COL))
    out_specs = (P(ROW + COL, None), P())
    return jax.shard_map(local, mesh=parts, in_specs=in_specs, out_specs=out_specs, check_vma=False)
```

```python
import functools
import math

import jax
import jax.numpy as jnp
from jax import lax
from jax.experimental import pallas as pl
from jax.experimental.pallas import tpu as pltpu
from jax.sharding import Mesh
from jax.sharding import PartitionSpec as P

TILE = 128


Z, Y, CHIP, CORE = "z", "y_hi", ("y_lo", "x"), "core"
ROW, COL, PLANE = (Z, Y), CHIP + (CORE,), (Y,) + CHIP
LIMIT = 32767.0


def exchange(blocks, axis):
    return lax.all_to_all(blocks, axis, split_axis=0, concat_axis=0, tiled=True)


def spread(block, axis):
    n = lax.axis_size(axis)
    return exchange(jnp.broadcast_to(block[None], (n,) + block.shape), axis)


def swap(block, axis):
    return lax.ppermute(block, axis, [(0, 1), (1, 0)])


def scatter_sum(whole, axis):
    n = lax.axis_size(axis)
    rows, columns = whole.shape
    return jnp.sum(exchange(whole.reshape(n, rows // n, columns), axis), axis=0)


def scatter_sum_16(pieces, axis):
    n, _, columns = pieces.shape
    top = jnp.max(jnp.abs(pieces), axis=1, keepdims=True)
    power = jnp.ceil(jnp.log2(jnp.maximum(top, 1e-30)) + 0.001)
    coded = jnp.round(pieces * (jnp.exp2(-power) * LIMIT)).astype(jnp.int16)
    powers = jnp.broadcast_to(power.astype(jnp.int16), (n, 8, columns))
    came = exchange(jnp.concatenate([coded, powers], axis=1), axis)
    unit = jnp.exp2(came[:, -1:].astype(jnp.float32)) * (1 / LIMIT)
    return jnp.sum(came[:, :-8].astype(jnp.float32) * unit, axis=0)


def chip_scatter_sum(whole):
    n = lax.axis_size(CHIP)
    rows, columns = whole.shape
    halves = whole.reshape(n, 2, rows // (2 * n), columns)
    core = lax.axis_index(CORE)
    mine = lax.dynamic_index_in_dim(halves, core, axis=1, keepdims=False)
    other = lax.dynamic_index_in_dim(halves, 1 - core, axis=1, keepdims=False)
    return scatter_sum_16(mine + swap(other, CORE), CHIP)


def chip_spread(block):
    mine = spread(block, CHIP)
    other = swap(mine, CORE)
    first = lax.axis_index(CORE) == 0
    both = jnp.stack([jnp.where(first, mine, other), jnp.where(first, other, mine)], axis=1)
    return both.reshape((-1,) + block.shape)


SUB = 8
LANES = 128
PANEL = 64
GROUP = 16


def eliminate(panel, first):
    height, width = panel.shape
    tiles = height // SUB
    rows = [panel[SUB * v : SUB * (v + 1)] for v in range(tiles)]
    sub = lax.broadcasted_iota(jnp.int32, (SUB, LANES), 0)

    def wide(a):
        return jnp.concatenate([a] * (width // LANES), axis=1)

    done = []
    for start in range(0, tiles, GROUP // SUB):
        at = first + start * SUB
        pivots = [jnp.zeros((SUB, LANES), jnp.float32) for _ in range(GROUP // SUB)]
        columns = {
            v: [jnp.broadcast_to(rows[v][:, at + k : at + k + 1], (SUB, LANES)) for k in range(GROUP)]
            for v in range(start, tiles)
        }
        for k in range(GROUP):
            i, r = divmod(k, SUB)
            t = start + i
            pivot = jnp.broadcast_to(columns[t][k][r : r + 1], (SUB, LANES))
            inverse = 1.0 / pivot
            pivots[i] = jnp.where(sub == r, pivot, pivots[i])
            row = jnp.broadcast_to(rows[t][r : r + 1], (SUB, width))
            heads = [jnp.broadcast_to(columns[t][l][r : r + 1], (SUB, LANES)) for l in range(k + 1, GROUP)]
            for v in range(t, tiles):
                times = columns[v][k] * inverse
                if v == t:
                    times = jnp.where(sub > r, times, 0.0)
                rows[v] = rows[v] - wide(times) * row
                for l in range(k + 1, GROUP):
                    columns[v][l] = columns[v][l] - times * heads[l - k - 1]
        done += [rows[start + i] * wide(lax.rsqrt(pivots[i])) for i in range(GROUP // SUB)]
    return jnp.concatenate(done, axis=0)


def cholesky_qr_kernel(scale, gram_ref, right_ref, factor_ref, basis_ref, work):
    n, size = right_ref.shape
    work[:, :size] = gram_ref[...]
    right = right_ref[...]
    if n < LANES:
        right = jnp.concatenate([right, jnp.zeros((LANES - n, size), jnp.float32)], axis=0)
    work[:, size:] = right.T
    for low in range(0, size, PANEL):
        high = low + PANEL
        panel = eliminate(work[low:high, :], low)
        work[low:high, :] = panel
        if high < size:
            base = high // LANES * LANES
            change = lax.dot_general(
                panel[:, base:size],
                panel,
                (((0,), (0,)), ((), ())),
                precision=lax.Precision.HIGHEST,
                preferred_element_type=jnp.float32,
            )
            work[high:, :] = work[high:, :] - change[high - base :]
    at_row = lax.broadcasted_iota(jnp.int32, (size, size), 0)
    at_column = lax.broadcasted_iota(jnp.int32, (size, size), 1)
    factor_ref[...] = jnp.where(at_row <= at_column, work[:, :size], 0.0)
    basis_ref[...] = work[:, size:].T[:n] * scale


def cholesky_qr(gram, right, scale):
    vmem = pl.BlockSpec(memory_space=pltpu.VMEM)
    size = gram.shape[0]
    return pl.pallas_call(
        functools.partial(cholesky_qr_kernel, scale),
        out_shape=(
            jax.ShapeDtypeStruct((size, size), jnp.float32),
            jax.ShapeDtypeStruct(right.shape, jnp.float32),
        ),
        in_specs=[vmem, vmem],
        out_specs=(vmem, vmem),
        scratch_shapes=[pltpu.VMEM((size, size + LANES), jnp.float32)],
        name="cholesky_qr",
    )(gram, right)


def masked(pmi, tile_mask):
    rows, cols = pmi.shape
    scaled = tile_mask.astype(jnp.bfloat16)[:, None, :, None]
    return (pmi.reshape(rows // TILE, TILE, cols // TILE, TILE) * scaled).reshape(rows, cols)


def local(pmi, tile_mask, probe):
    rows, cols = pmi.shape
    again, mask_again = lax.optimization_barrier((pmi, tile_mask))
    probe_full = chip_spread(probe.T).reshape(-1, cols)
    k = probe_full.shape[0]
    partial_value = lax.dot_general(
        masked(pmi, tile_mask), probe_full, (((1,), (1,)), ((), ())), preferred_element_type=jnp.float32
    )
    sketch_rows = scatter_sum_16(partial_value.reshape(lax.axis_size(Z), -1, k), Z)
    sketch_rows = (sketch_rows + swap(sketch_rows, Y)).astype(jnp.bfloat16)
    sketch = spread(sketch_rows, Z).reshape(rows, k)
    image = lax.dot_general(
        masked(again, mask_again), sketch, (((0,), (0,)), ((), ())), preferred_element_type=jnp.float32
    )
    mine = chip_scatter_sum(image)
    gram_part = jnp.dot(
        mine.T, mine, precision=lax.Precision.HIGHEST, preferred_element_type=jnp.float32
    )
    gram_rows = jnp.sum(spread(scatter_sum(gram_part, PLANE), Z), axis=0)
    gram_rows = gram_rows + swap(gram_rows, CORE)
    gram = spread(gram_rows, PLANE).reshape(k, k)
    scale = math.sqrt(cols * lax.axis_size(ROW))
    factor, basis = cholesky_qr(gram, mine, scale)
    return (basis, factor)


def solution(mesh):
    sizes = (mesh.shape["row"] // 2, 2, 4, mesh.shape["col"] // 8, 2)
    parts = Mesh(mesh.devices.reshape(sizes), ROW + COL)
    in_specs = (P(COL, ROW), P(COL, ROW), P(ROW, COL))
    out_specs = (P(ROW + COL, None), P())
    return jax.shard_map(local, mesh=parts, in_specs=in_specs, out_specs=out_specs, check_vma=False)
```

```python
import functools
import math

import jax
import jax.numpy as jnp
from jax import lax
from jax.experimental import pallas as pl
from jax.experimental.pallas import tpu as pltpu
from jax.sharding import Mesh
from jax.sharding import PartitionSpec as P

TILE = 128


Z, Y, CHIP, CORE = "z", "y_hi", ("y_lo", "x"), "core"
ROW, COL, PLANE = (Z, Y), CHIP + (CORE,), (Y,) + CHIP
LIMIT = 32767.0
LEAST, STEPS, OCTAVES = 4096.0, 322.0, 81.0


def exchange(blocks, axis):
    return lax.all_to_all(blocks, axis, split_axis=0, concat_axis=0, tiled=True)


def spread(block, axis):
    n = lax.axis_size(axis)
    return exchange(jnp.broadcast_to(block[None], (n,) + block.shape), axis)


def swap(block, axis):
    return lax.ppermute(block, axis, [(0, 1), (1, 0)])


def scatter_sum(whole, axis):
    n = lax.axis_size(axis)
    rows, columns = whole.shape
    return jnp.sum(exchange(whole.reshape(n, rows // n, columns), axis), axis=0)


def scatter_sum_16(pieces, axis):
    n, _, columns = pieces.shape
    top = jnp.max(jnp.abs(pieces), axis=1, keepdims=True)
    power = jnp.ceil(jnp.log2(jnp.maximum(top, 1e-30)) + 0.001)
    coded = jnp.round(pieces * (jnp.exp2(-power) * LIMIT)).astype(jnp.int16)
    powers = jnp.broadcast_to(power.astype(jnp.int16), (n, 8, columns))
    came = exchange(jnp.concatenate([coded, powers], axis=1), axis)
    unit = jnp.exp2(came[:, -1:].astype(jnp.float32)) * (1 / LIMIT)
    return jnp.sum(came[:, :-8].astype(jnp.float32) * unit, axis=0)


def scatter_sum_marked(pieces, axis):
    top = jnp.max(jnp.abs(pieces), axis=1, keepdims=True)
    level = jnp.ceil((jnp.log2(jnp.maximum(top, 1e-30)) + OCTAVES) * STEPS)
    mark = LEAST + jnp.clip(level, 0.0, LIMIT - LEAST)
    size = jnp.exp2((mark - LEAST) * (1 / STEPS) - OCTAVES)
    coded = jnp.clip(jnp.round(pieces * (mark / size)), -mark, mark)
    coded = jnp.where(jnp.abs(pieces) >= top, jnp.sign(pieces) * mark, coded)
    came = exchange(coded.astype(jnp.int16), axis).astype(jnp.float32)
    mark = jnp.max(jnp.abs(came), axis=1, keepdims=True)
    size = jnp.exp2(jnp.maximum(mark - LEAST, 0.0) * (1 / STEPS) - OCTAVES)
    return jnp.sum(came * (size / jnp.maximum(mark, 1.0)), axis=0)


def chip_scatter_sum(whole):
    n = lax.axis_size(CHIP)
    rows, columns = whole.shape
    halves = whole.reshape(n, 2, rows // (2 * n), columns)
    core = lax.axis_index(CORE)
    mine = lax.dynamic_index_in_dim(halves, core, axis=1, keepdims=False)
    other = lax.dynamic_index_in_dim(halves, 1 - core, axis=1, keepdims=False)
    return scatter_sum_16(mine + swap(other, CORE), CHIP)


def chip_spread(block):
    mine = spread(block, CHIP)
    other = swap(mine, CORE)
    first = lax.axis_index(CORE) == 0
    both = jnp.stack([jnp.where(first, mine, other), jnp.where(first, other, mine)], axis=1)
    return both.reshape((-1,) + block.shape)


SUB = 8
LANES = 128
PANEL = 64
GROUP = 16


def eliminate(panel, first):
    height, width = panel.shape
    tiles = height // SUB
    rows = [panel[SUB * v : SUB * (v + 1)] for v in range(tiles)]
    sub = lax.broadcasted_iota(jnp.int32, (SUB, LANES), 0)

    def wide(a):
        return jnp.concatenate([a] * (width // LANES), axis=1)

    done = []
    for start in range(0, tiles, GROUP // SUB):
        at = first + start * SUB
        pivots = [jnp.zeros((SUB, LANES), jnp.float32) for _ in range(GROUP // SUB)]
        columns = {
            v: [jnp.broadcast_to(rows[v][:, at + k : at + k + 1], (SUB, LANES)) for k in range(GROUP)]
            for v in range(start, tiles)
        }
        for k in range(GROUP):
            i, r = divmod(k, SUB)
            t = start + i
            pivot = jnp.broadcast_to(columns[t][k][r : r + 1], (SUB, LANES))
            inverse = 1.0 / pivot
            pivots[i] = jnp.where(sub == r, pivot, pivots[i])
            row = jnp.broadcast_to(rows[t][r : r + 1], (SUB, width))
            heads = [jnp.broadcast_to(columns[t][l][r : r + 1], (SUB, LANES)) for l in range(k + 1, GROUP)]
            for v in range(t, tiles):
                times = columns[v][k] * inverse
                if v == t:
                    times = jnp.where(sub > r, times, 0.0)
                rows[v] = rows[v] - wide(times) * row
                for l in range(k + 1, GROUP):
                    columns[v][l] = columns[v][l] - times * heads[l - k - 1]
        done += [rows[start + i] * wide(lax.rsqrt(pivots[i])) for i in range(GROUP // SUB)]
    return jnp.concatenate(done, axis=0)


def cholesky_qr_kernel(scale, gram_ref, right_ref, factor_ref, basis_ref, work):
    n, size = right_ref.shape
    work[:, :size] = gram_ref[...]
    right = right_ref[...]
    if n < LANES:
        right = jnp.concatenate([right, jnp.zeros((LANES - n, size), jnp.float32)], axis=0)
    work[:, size:] = right.T
    for low in range(0, size, PANEL):
        high = low + PANEL
        panel = eliminate(work[low:high, :], low)
        work[low:high, :] = panel
        if high < size:
            base = high // LANES * LANES
            change = lax.dot_general(
                panel[:, base:size],
                panel,
                (((0,), (0,)), ((), ())),
                precision=lax.Precision.HIGHEST,
                preferred_element_type=jnp.float32,
            )
            work[high:, :] = work[high:, :] - change[high - base :]
    at_row = lax.broadcasted_iota(jnp.int32, (size, size), 0)
    at_column = lax.broadcasted_iota(jnp.int32, (size, size), 1)
    factor_ref[...] = jnp.where(at_row <= at_column, work[:, :size], 0.0)
    basis_ref[...] = work[:, size:].T[:n] * scale


def cholesky_qr(gram, right, scale):
    vmem = pl.BlockSpec(memory_space=pltpu.VMEM)
    size = gram.shape[0]
    return pl.pallas_call(
        functools.partial(cholesky_qr_kernel, scale),
        out_shape=(
            jax.ShapeDtypeStruct((size, size), jnp.float32),
            jax.ShapeDtypeStruct(right.shape, jnp.float32),
        ),
        in_specs=[vmem, vmem],
        out_specs=(vmem, vmem),
        scratch_shapes=[pltpu.VMEM((size, size + LANES), jnp.float32)],
        name="cholesky_qr",
    )(gram, right)


def masked(pmi, tile_mask):
    rows, cols = pmi.shape
    scaled = tile_mask.astype(jnp.bfloat16)[:, None, :, None]
    return (pmi.reshape(rows // TILE, TILE, cols // TILE, TILE) * scaled).reshape(rows, cols)


def local(pmi, tile_mask, probe):
    rows, cols = pmi.shape
    again, mask_again = lax.optimization_barrier((pmi, tile_mask))
    probe_full = chip_spread(probe.T).reshape(-1, cols)
    k = probe_full.shape[0]
    partial_value = lax.dot_general(
        masked(pmi, tile_mask), probe_full, (((1,), (1,)), ((), ())), preferred_element_type=jnp.float32
    )
    sketch_rows = scatter_sum_marked(partial_value.reshape(lax.axis_size(Z), -1, k), Z)
    sketch_rows = (sketch_rows + swap(sketch_rows, Y)).astype(jnp.bfloat16)
    sketch = spread(sketch_rows, Z).reshape(rows, k)
    image = lax.dot_general(
        masked(again, mask_again), sketch, (((0,), (0,)), ((), ())), preferred_element_type=jnp.float32
    )
    mine = chip_scatter_sum(image)
    gram_part = jnp.dot(
        mine.T, mine, precision=lax.Precision.HIGHEST, preferred_element_type=jnp.float32
    )
    gram_rows = jnp.sum(spread(scatter_sum(gram_part, PLANE), Z), axis=0)
    gram_rows = gram_rows + swap(gram_rows, CORE)
    gram = spread(gram_rows, PLANE).reshape(k, k)
    scale = math.sqrt(cols * lax.axis_size(ROW))
    factor, basis = cholesky_qr(gram, mine, scale)
    return (basis, factor)


def solution(mesh):
    sizes = (mesh.shape["row"] // 2, 2, 4, mesh.shape["col"] // 8, 2)
    parts = Mesh(mesh.devices.reshape(sizes), ROW + COL)
    in_specs = (P(COL, ROW), P(COL, ROW), P(ROW, COL))
    out_specs = (P(ROW + COL, None), P())
    return jax.shard_map(local, mesh=parts, in_specs=in_specs, out_specs=out_specs, check_vma=False)
```
